128 devices in a mesh: dp: 8 (over y_hi, z), tensor: 16 (over x, y_lo, core).
Axes of the slice: x: 4, y: 4 (y_hi: 2, y_lo: 2; y = y_hi * 2 + y_lo), z: 4, core: 2. Of those that a mesh axis runs over, the one named last changes fastest.
Arguments:
- cotangent: bfloat16 [16384, 4096], P(('dp', 'tensor')), may hold values from -24 to 24
- gate_in: bfloat16 [16384, 14336], P('dp', 'tensor'), may hold values from -6 to 6
- up_in: bfloat16 [16384, 14336], P('dp', 'tensor'), may hold values from -6 to 6
- down_weight: bfloat16 [14336, 4096], P('tensor'), may hold values from -0.046875 to 0.046875
- lengths: int32 [8], P('dp'), may hold values from 1024 to 2048, as said below
- remasked: int32 [8, 512], P('dp'), may hold values from 0 to 2047, as said below
Outputs:
- gate_grad: bfloat16 [16384, 14336], P('dp', 'tensor')
- up_grad: bfloat16 [16384, 14336], P('dp', 'tensor')
- weight_grad: float32 [14336, 4096], P('tensor', 'dp')
The draws below stay inside these ranges and needn't reach their ends.
Inputs may be any that keep to these rules, and one draw needn't show every extreme that they name: `remasked`: each row holds 512 distinct positions; 0 and 2047 are in every row. `lengths`: some canvas has length 2048 and some other one 2048 // 2.
All inputs are finite; a program needn't handle non-finite values.
Results may differ from the reference program's by a relative error of at most 0.013.
Values may be sent and summed in bfloat16 or wider, within the bound.
No kernel may reach another device: no remote copies, remote signals or barrier semaphores. Data moves between devices by JAX's collectives and lax.ppermute only.
A program may use at most 128 MiB of HBM per device.

```python
import jax
import jax.numpy as jnp
from jax import lax

D = 4096
FF = 14336
SEQ = 2048
REM = 512
ROWS = 16384
N_DP = 8


def draw_lengths(key, part):
    key = jax.random.fold_in(key, 11)
    first, second = jax.random.split(key)
    base = jax.random.randint(first, (N_DP,), SEQ // 2, SEQ + 1)
    top_index = jax.random.randint(second, (), 0, N_DP)
    low_index = (top_index + 1) % N_DP
    places = jnp.arange(N_DP)
    base = jnp.where(places == top_index, SEQ, jnp.where(places == low_index, SEQ // 2, base))
    return base.astype(jnp.int32)


def one_canvas(key):
    inner = jax.random.permutation(key, SEQ - 2)[:REM - 2] + 1
    edges_low = jnp.zeros((1,), jnp.int32)
    edges_high = jnp.full((1,), SEQ - 1, jnp.int32)
    return jnp.concatenate([edges_low, inner.astype(jnp.int32), edges_high])


def draw_remasked(key, part):
    key = jax.random.fold_in(key, 12)
    keys = jax.random.split(key, N_DP)
    return jax.vmap(one_canvas)(keys).astype(jnp.int32)


def with_spikes(values, stream_key, source, target, shards_of, factor):
    owner, partner = [(jnp.arange(values.shape[position]) // (values.shape[position] // shards_of)).reshape([-1 if axis == position else 1 for axis in range(values.ndim)]) for position in (source, target)]
    chosen = jax.random.permutation(stream_key, shards_of)[partner]
    strong = (owner == chosen) | (owner == (partner + shards_of // 2) % shards_of)
    return jnp.where(strong, factor * values, values)


def levels(own_key, dims, pieces, least, largest):
    loudness, own = 1.0, jax.random.fold_in(own_key, 6)
    for dim, parts in pieces:
        steps = jnp.exp(jax.random.uniform(jax.random.fold_in(own, dim), (parts,), jnp.float32, least / len(pieces), largest / len(pieces)))
        loudness = loudness * jnp.repeat(steps, dims[dim] // parts).reshape([-1 if axis == dim else 1 for axis in range(len(dims))])
    return loudness


def gaussian(key, extent, deviation, reach, shards=(), kind=jnp.bfloat16):
    array = jax.random.normal(key, extent, jnp.float32) * deviation
    if len(shards) > 0:
        array = levels(key, extent, shards, -0.22, 0.18) * array
    return jnp.clip(array, min=-reach, max=reach).astype(kind)


def gaussian_with(own_key, shape, deviation, reach, cuts, heavy, held_as=jnp.bfloat16):
    array = deviation * jax.random.normal(own_key, shape, jnp.float32)
    if cuts:
        array = array * levels(own_key, shape, cuts, -0.22, 0.18)
    return jnp.clip(with_spikes(array, jax.random.fold_in(own_key, 3), *heavy), -reach, reach).astype(held_as)


def setup_inputs(seed: int = 0) -> dict:
    streams_of = jax.random.split(jax.random.key(seed), 7)
    cotangent = gaussian_with(streams_of[0], (ROWS, D), 1.0, 24.0, ((0, 128),), (0, 1, 128, 5.5))
    gate_in = gaussian(streams_of[1], (ROWS, FF), 1.5, 6.0, ((0, 8), (1, 16)))
    up_in = gaussian(streams_of[2], (ROWS, FF), 1.0, 6.0, ((0, 8), (1, 16)))
    down_weight = gaussian(streams_of[3], (FF, D), FF ** -0.5, 0.046875, ((0, 16),))
    lengths = draw_lengths(jax.random.fold_in(streams_of[6], 71), 0)
    remasked = draw_remasked(jax.random.fold_in(streams_of[6], 71), 0)
    return {"cotangent": cotangent, "gate_in": gate_in, "up_in": up_in, "down_weight": down_weight, "lengths": lengths, "remasked": remasked}


def reference(cotangent, gate_in, up_in, down_weight, lengths, remasked):
    positions = jnp.arange(SEQ, dtype=jnp.int32)
    valid = positions[None, :] < lengths[:, None]
    marked = jnp.any(positions[None, :, None] == remasked[:, None, :], axis=2)
    loss_weight = jnp.where(valid, jnp.where(marked, 2.0, 1.0), 0.0).astype(jnp.bfloat16)
    scaled = cotangent.reshape(N_DP, SEQ, D) * loss_weight[:, :, None]
    gates = gate_in.reshape(N_DP, SEQ, FF)
    ups = up_in.reshape(N_DP, SEQ, FF)

    def canvas(total, items):
        rows, gate, upper = items
        gate_f = gate.astype(jnp.float32)
        upper_f = upper.astype(jnp.float32)
        sig = jax.nn.sigmoid(gate_f)
        hidden = (gate_f * sig * upper_f).astype(jnp.bfloat16)
        hidden_grad = jnp.dot(rows, down_weight.T, preferred_element_type=jnp.float32)
        partial_term = jnp.dot(hidden.T, rows, preferred_element_type=jnp.float32).astype(jnp.bfloat16)
        partial_term = lax.optimization_barrier(partial_term)
        total = total + partial_term.astype(jnp.float32)
        up_grad = (hidden_grad * gate_f * sig).astype(jnp.bfloat16)
        gate_grad = (hidden_grad * upper_f * sig * (1.0 + gate_f * (1.0 - sig))).astype(jnp.bfloat16)
        return total, (gate_grad, up_grad)

    start = jnp.zeros((FF, D), jnp.float32)
    weight_grad, grads = lax.scan(canvas, start, (scaled, gates, ups))
    gate_grad = grads[0].reshape(N_DP * SEQ, FF)
    up_grad = grads[1].reshape(N_DP * SEQ, FF)
    return gate_grad, up_grad, weight_grad
```

```python
import jax
import jax.numpy as jnp
from jax import lax
from jax.experimental import pallas as pl
from jax.experimental.pallas import tpu as pltpu
from jax.sharding import PartitionSpec as P

F32 = jnp.float32
BF16 = jnp.bfloat16
VMEM_LIMIT = 34 * 1024 * 1024

CHUNKS = (((2, 1),), ((1, 1), (-1, 1)), ((2, 0), (0, 1)), ((1, 0), (-1, 0)), ((0, 0),))
SHARDS = (
    (0, 0, 0), (0, 1, 0), (0, 0, 1), (0, 1, 1),
    (-1, 0, 0), (-1, 1, 0), (-1, 0, 1), (-1, 1, 1),
    (2, 0, 0), (2, 1, 0),
    (1, 0, 1), (1, 1, 1), (1, 0, 0), (1, 1, 0),
    (2, 0, 1), (2, 1, 1),
)
N_PIECES = 8
PIECE = 256
UNIT = 512
ROWS = N_PIECES * PIECE


def pairs(move):
    sizes = (2, 4, 4, 2, 2)

    def index(at):
        n = 0
        for i, size in zip(at, sizes):
            n = n * size + i % size
        return n

    out = []
    for n in range(128):
        rest, at = n, []
        for size in reversed(sizes):
            at.append(rest % size)
            rest //= size
        at = tuple(reversed(at))
        out.append((index(at), index(move(*at))))
    return out


def move(v, to, name):
    with jax.named_scope(name):
        return lax.ppermute(v, ("dp", "tensor"), pairs(to))


def along_x(v, name):
    return move(v, lambda yh, z, x, yl, c: (yh, z, x + 1 - 2 * c, yl, c), name)


def along_y(v, name):
    return move(v, lambda yh, z, x, yl, c: (yh, z, x, yl + 1, c), name)


def across_cores(v, name):
    return move(v, lambda yh, z, x, yl, c: (yh, z, x, yl, c + 1), name)


def along_z(v, step, name):
    return move(v, lambda yh, z, x, yl, c: (yh, z + step * (1 - 2 * c), x, yl, c), name)


def across_y(v, name):
    return move(v, lambda yh, z, x, yl, c: (yh + 1, z, x, yl, c), name)


def after(v, *others):
    return lax.optimization_barrier((v, *others))[0]


def after_all(values, *others):
    return lax.optimization_barrier((*values, *others))[: len(values)]


def params():
    return pltpu.CompilerParams(vmem_limit_bytes=VMEM_LIMIT)


def hbm(values):
    return [pltpu.with_memory_space_constraint(v, pltpu.HBM) for v in values]


def vmem(values):
    return [pltpu.with_memory_space_constraint(v, pltpu.VMEM) for v in values]


IN_HBM = pl.BlockSpec(memory_space=pltpu.HBM)
IN_VMEM = pl.BlockSpec(memory_space=pltpu.VMEM)


def slices_kernel(widths, dests, cotangent, *refs):
    outs, sems = refs[:-1], refs[-1]
    copies = []
    u = 0
    for out, n in zip(outs, widths):
        for k in range(n):
            copies.append(
                pltpu.make_async_copy(
                    cotangent.at[:, pl.ds(pl.multiple_of(dests[u] * UNIT, UNIT), UNIT)],
                    out.at[:, k * UNIT : (k + 1) * UNIT],
                    sems.at[u],
                )
            )
            u += 1
    for copy in copies:
        copy.start()
    for copy in copies:
        copy.wait()


def slices(dests, cotangent):
    rows = cotangent.shape[0]
    widths = [len(units) for units in CHUNKS]
    return pl.pallas_call(
        lambda *refs: slices_kernel(widths, *refs),
        grid_spec=pltpu.PrefetchScalarGridSpec(
            num_scalar_prefetch=1,
            grid=(),
            in_specs=[IN_HBM],
            out_specs=[IN_HBM] * len(widths),
            scratch_shapes=[pltpu.SemaphoreType.DMA((sum(widths),))],
        ),
        out_shape=[jax.ShapeDtypeStruct((rows, n * UNIT), BF16) for n in widths],
        compiler_params=params(),
        cost_estimate=pl.CostEstimate(
            flops=0, bytes_accessed=4 * cotangent.size, transcendentals=0
        ),
        name="slices",
    )(dests, *hbm([cotangent]))


GROUP = 4


def factors_kernel(order, lengths, remasked, *refs):
    gates, uppers = refs[:GROUP], refs[GROUP : 2 * GROUP]
    hidden_t, up_factor, gate_factor = refs[2 * GROUP :]
    rows = gates[0].shape[0]
    marks = remasked[...]
    for k in range(GROUP):
        shard = pl.program_id(0) * GROUP + k
        start = order[shard] * rows
        at = start + lax.broadcasted_iota(jnp.int32, (rows, marks.shape[1]), 0)
        marked = jnp.max(jnp.where(at == marks, 1.0, 0.0), axis=1, keepdims=True)
        position = start + lax.broadcasted_iota(jnp.int32, (rows, 1), 0)
        weight = jnp.where(position < lengths[0], 1.0 + marked, 0.0)
        gate_f = gates[k][...].astype(F32)
        upper_f = uppers[k][...].astype(F32)
        sigma = 0.5 + 0.5 * jnp.tanh(0.5 * gate_f)
        weighted = gate_f * sigma * weight
        at = pl.ds(pl.multiple_of(shard * rows, rows), rows)
        hidden_t[:, at] = (weighted * upper_f).astype(BF16).T
        up_factor[at] = weighted.astype(BF16)
        slope = (sigma * weight) * (1.0 + gate_f * (1.0 - sigma))
        gate_factor[at] = (upper_f * slope).astype(BF16)


def factors(order, lengths, remasked, gate, upper):
    rows, width = gate.shape
    block = rows // 16
    blocks = [
        pl.BlockSpec((block, width), lambda i, order, lengths, k=k: (order[i * GROUP + k], 0))
        for k in range(GROUP)
    ]
    return pl.pallas_call(
        factors_kernel,
        grid_spec=pltpu.PrefetchScalarGridSpec(
            num_scalar_prefetch=2,
            grid=(16 // GROUP,),
            in_specs=[pl.BlockSpec(remasked.shape, lambda i, order, lengths: (0, 0))] + blocks * 2,
            out_specs=[IN_VMEM] * 3,
        ),
        out_shape=[
            pltpu.VMEM((width, rows), BF16),
            pltpu.VMEM((rows, width), BF16),
            pltpu.VMEM((rows, width), BF16),
        ],
        compiler_params=params(),
        cost_estimate=pl.CostEstimate(
            flops=30 * rows * width, bytes_accessed=4 * rows * width, transcendentals=rows * width
        ),
        name="factors",
    )(order, lengths, remasked, *hbm([gate] * GROUP), *hbm([upper] * GROUP))


def weight_kernel(n, flip, hidden_t, *refs):
    pieces, outs = refs[:N_PIECES], refs[N_PIECES : N_PIECES + n]
    chunk, results, sems, out_sems = refs[N_PIECES + n :]
    cols = chunk.shape[2]
    per_unit = UNIT // cols

    def fetch(j):
        at = jnp.bitwise_xor(j // per_unit, flip[0]) * UNIT + j % per_unit * cols
        return [
            pltpu.make_async_copy(
                piece.at[:, pl.ds(pl.multiple_of(at, cols), cols)],
                chunk.at[j, i * PIECE : (i + 1) * PIECE],
                sems.at[j, i],
            )
            for i, piece in enumerate(pieces)
        ]

    copies = [fetch(j) for j in range(n * per_unit)]
    for some in copies:
        for copy in some:
            copy.start()
    stores = []
    for j, some in enumerate(copies):
        for copy in some:
            copy.wait()
        total = jnp.dot(hidden_t[...], chunk[j], preferred_element_type=F32)
        results[j] = total.astype(BF16)
        at = j % per_unit * cols
        stores.append(
            pltpu.make_async_copy(
                results.at[j], outs[j // per_unit].at[:, at : at + cols], out_sems.at[j]
            )
        )
        stores[-1].start()
    for store in stores:
        store.wait()


def weight_terms(flip, hidden_t, pieces):
    ff, rows = hidden_t.shape
    n = pieces[0].shape[1] // UNIT
    cols = 256
    blocks = n * UNIT // cols
    return pl.pallas_call(
        lambda *refs: weight_kernel(n, *refs),
        grid_spec=pltpu.PrefetchScalarGridSpec(
            num_scalar_prefetch=1,
            grid=(),
            in_specs=[IN_VMEM] + [IN_HBM] * N_PIECES,
            out_specs=[IN_HBM] * n,
            scratch_shapes=[
                pltpu.VMEM((blocks, rows, cols), BF16),
                pltpu.VMEM((blocks, ff, cols), BF16),
                pltpu.SemaphoreType.DMA((blocks, N_PIECES)),
                pltpu.SemaphoreType.DMA((blocks,)),
            ],
        ),
        out_shape=[jax.ShapeDtypeStruct((ff, UNIT), BF16)] * n,
        compiler_params=params(),
        cost_estimate=pl.CostEstimate(
            flops=2 * ff * rows * n * UNIT,
            bytes_accessed=2 * (rows * n * UNIT + ff * n * UNIT),
            transcendentals=0,
        ),
        name="weight_terms",
    )(flip, *vmem([hidden_t]), *hbm(pieces))


BLOCK = 512


def load_parts(units, first, dests, chunks, weight, chunk, weights, sems, weight_sems):
    rows = []
    for block in range(ROWS // BLOCK):
        copies = []
        for half in range(BLOCK // PIECE):
            piece = block * (BLOCK // PIECE) + half
            start = 0
            for k, (pieces, n) in enumerate(zip(chunks, units)):
                copies.append(
                    pltpu.make_async_copy(
                        pieces[piece],
                        chunk.at[piece * PIECE : (piece + 1) * PIECE, start : start + n * UNIT],
                        sems.at[piece, k],
                    )
                )
                start += n * UNIT
        rows.append(copies)
    columns = [
        pltpu.make_async_copy(
            weight.at[:, pl.ds(pl.multiple_of(dests[first + u] * UNIT, UNIT), UNIT)],
            weights.at[:, u * UNIT : (u + 1) * UNIT],
            weight_sems.at[u],
        )
        for u in range(sum(units))
    ]
    for copy in rows[0] + columns + [copy for copies in rows[1:] for copy in copies]:
        copy.start()
    return rows, columns


def times_t(a, b):
    return lax.dot_general(a, b, (((1,), (1,)), ((), ())), preferred_element_type=F32)


def split(refs, units):
    refs = list(refs)
    chunks = [[refs.pop(0) for _ in range(N_PIECES)] for _ in units]
    return chunks, refs


def first_grad_kernel(units, order, dests, *refs):
    chunks, (weight, out, *scratch) = split(refs, units)
    rows, columns = load_parts(units, 0, dests, chunks, weight, *scratch)
    chunk, weights = scratch[:2]
    for copy in columns:
        copy.wait()
    for block, copies in enumerate(rows):
        for copy in copies:
            copy.wait()
        at = slice(block * BLOCK, (block + 1) * BLOCK)
        out[at] = times_t(chunk[at], weights[...])


def last_grad_kernel(units, first, order, dests, *refs):
    chunks, (weight, before, up_factor, gate_factor, gate_out, up_out, *scratch) = split(refs, units)
    *scratch, gate_buf, up_buf, out_sems = scratch
    rows, columns = load_parts(units, first, dests, chunks, weight, *scratch)
    chunk, weights = scratch[:2]
    for copy in columns:
        copy.wait()
    shard = ROWS // 16
    stores = []
    for block, copies in enumerate(rows):
        for copy in copies:
            copy.wait()
        at = slice(block * BLOCK, (block + 1) * BLOCK)
        total = before[at] + times_t(chunk[at], weights[...])
        gate_buf[at] = (total * gate_factor[at].astype(F32)).astype(BF16)
        up_buf[at] = (total * up_factor[at].astype(F32)).astype(BF16)
        for index in range(block * BLOCK // shard, (block + 1) * BLOCK // shard):
            for which, (buf, out) in enumerate(((gate_buf, gate_out), (up_buf, up_out))):
                stores.append(
                    pltpu.make_async_copy(
                        buf.at[index * shard : (index + 1) * shard],
                        out.at[pl.ds(pl.multiple_of(order[index] * shard, shard), shard)],
                        out_sems.at[which, index],
                    )
                )
                stores[-1].start()
    for store in stores:
        store.wait()


def grad(order, dests, chunks, first, weight, rest=()):
    ff = weight.shape[0]
    units = tuple(pieces[0].shape[1] // UNIT for pieces in chunks)
    total = sum(units)
    scratch = [
        pltpu.VMEM((ROWS, UNIT * total), BF16),
        pltpu.VMEM((ff, UNIT * total), BF16),
        pltpu.SemaphoreType.DMA((N_PIECES, len(chunks))),
        pltpu.SemaphoreType.DMA((total,)),
    ]
    if rest:
        kernel = lambda *refs: last_grad_kernel(units, first, *refs)
        scratch += [pltpu.VMEM((ROWS, ff), BF16)] * 2
        scratch += [pltpu.SemaphoreType.DMA((2, 16))]
        out_specs = [IN_HBM] * 2
        out_shape = [jax.ShapeDtypeStruct((ROWS, ff), BF16)] * 2
    else:
        kernel = lambda *refs: first_grad_kernel(units, *refs)
        out_specs = IN_VMEM
        out_shape = pltpu.VMEM((ROWS, ff), F32)
    return pl.pallas_call(
        kernel,
        grid_spec=pltpu.PrefetchScalarGridSpec(
            num_scalar_prefetch=2,
            grid=(),
            in_specs=[IN_HBM] * (N_PIECES * len(chunks) + 1) + [IN_VMEM] * len(rest),
            out_specs=out_specs,
            scratch_shapes=scratch,
        ),
        out_shape=out_shape,
        compiler_params=params(),
        cost_estimate=pl.CostEstimate(
            flops=2 * ROWS * ff * total * UNIT,
            bytes_accessed=2 * (ROWS + ff) * total * UNIT,
            transcendentals=0,
        ),
        name="last_grad" if rest else "first_grad",
    )(order, dests, *hbm([p for pieces in chunks for p in pieces] + [weight]), *vmem(rest))


def local(cotangent, gate_in, up_in, down_weight, lengths, remasked):
    t = lax.axis_index("tensor")
    d = lax.axis_index("dp")
    x, yl, c = t // 4, (t // 2) % 2, t % 2
    yh, z = d // 4, d % 4
    way = 1 - 2 * c
    order = jnp.stack(
        [
            (((x + way * dx + 4) % 4) * 2 + (yl + dy) % 2) * 2 + (c + dc) % 2
            for dx, dy, dc in SHARDS
        ]
    ).astype(jnp.int32)
    dests = jnp.stack(
        [((yh + dy) % 2) * 4 + (z + dz) % 4 for units in CHUNKS for dz, dy in units]
    ).astype(jnp.int32)
    flip = c.astype(jnp.int32).reshape(1)
    straight = jnp.zeros((1,), jnp.int32)

    mines = slices(dests, cotangent)
    hidden_t, up_factor, gate_factor = factors(order, lengths, remasked, gate_in, up_in)

    pair, crossed = [], []
    partner = None
    for k, mine in enumerate(mines):
        if k == 1:
            mine = after(mine, crossed[0])
        elif k > 1:
            mine = after(mine, partner, crossed[k - 2])
        partner = along_y(mine, f"partner_{k}")
        pair.append(jnp.concatenate([mines[k], partner], axis=0))
        crossed.append(across_cores(pair[k], f"crossed_{k}"))

    queue = []

    def next_along_x(v, name, *others):
        if len(queue) >= 2:
            others = (*others, queue[-2])
        queue.append(along_x(after(v, *others) if others else v, name))
        return queue[-1]

    def gather(k, first=(), second=(), third=()):
        one = next_along_x(pair[k], f"near_own_{k}", *first)
        two = next_along_x(crossed[k], f"near_crossed_{k}", *second)
        three = next_along_x(one, f"far_{k}", *third)
        swapped = [across_cores(v, f"swap{i}_{k}") for i, v in enumerate((one, two, three))]
        return (pair[k], crossed[k], one, two, three, *swapped)

    def add(*terms):
        return sum(term.astype(F32) for term in terms)

    chunk0 = gather(0, third=(hidden_t,))
    chunk1 = gather(1)
    (far,) = weight_terms(straight, hidden_t, chunk0)
    relayed = along_z(far, 1, "relay_0")
    chunk2 = gather(2, first=(far,), third=(relayed,))
    plus, minus = weight_terms(flip, hidden_t, chunk1)
    got_minus = along_z(minus, -1, "back_0")
    got_plus = along_z(add(plus, relayed).astype(BF16), 1, "forth_0")
    chunk3 = gather(3, second=(minus,))
    far, other = weight_terms(straight, hidden_t, chunk2)
    relayed = along_z(far, 1, "relay_1")
    chunk4 = gather(4, second=(far,))
    sums = grad(order, dests, [chunk0, chunk1, after_all(chunk2, far)], 0, down_weight)
    got_other = across_y(add(other, got_minus, got_plus).astype(BF16), "across_y")
    plus, minus = weight_terms(flip, after(hidden_t, sums), chunk3)
    got_minus = along_z(minus, -1, "back_1")
    got_plus = along_z(add(plus, relayed).astype(BF16), 1, "forth_1")
    (own,) = weight_terms(straight, hidden_t, chunk4)
    gate_grad, up_grad = grad(
        order, dests, [chunk3, chunk4], 5, down_weight, (after(sums, own), up_factor, gate_factor)
    )
    return (gate_grad, up_grad, add(own, got_minus, got_plus, got_other))


def solution(mesh):
    return jax.shard_map(
        local,
        mesh=mesh,
        in_specs=(
            P(("dp", "tensor"), None),
            P("dp", "tensor"),
            P("dp", "tensor"),
            P("tensor", None),
            P("dp"),
            P("dp", None),
        ),
        out_specs=(P("dp", "tensor"), P("dp", "tensor"), P("tensor", "dp")),
        check_vma=False,
    )
```

```python
import jax
import jax.numpy as jnp
from jax import lax
from jax.experimental import pallas as pl
from jax.experimental.pallas import tpu as pltpu
from jax.sharding import PartitionSpec as P

F32 = jnp.float32
BF16 = jnp.bfloat16
VMEM_LIMIT = 16 * 1024 * 1024

CHUNKS = (
    ((2, 1, 0, 512),),
    ((1, 1, 0, 512), (-1, 1, 0, 512)),
    ((2, 0, 0, 512), (0, 1, 0, 512)),
    ((1, 0, 0, 512), (-1, 0, 0, 512)),
    ((0, 0, 0, 512),),
)
GROUPS = ((0, 1), (2,), (3, 4))
WAITS = {
    "o": ("r_1", "w_3"),
    "f_0": ("e",),
    "f_1": ("w_0",),
    "f_2": ("h_0_0", "t_1", "w_1"),
    "f_3": ("w_2",),
    "f_4": ("g_0",),
    "h_0_0": ("w_1",),
    "h_0_1": ("w_1",),
    "h_1_0": ("w_2",),
    "h_1_1": ("w_2",),
    "h_2_0": ("w_3",),
    "m_1": ("f_0",),
    "m_2": ("f_1", "r_0"),
    "m_3": ("f_2",),
    "m_4": ("f_3", "t_3"),
    "n_1": ("m_0", "y_1"),
    "n_2": ("m_1", "y_2"),
    "n_3": ("h_0_1", "m_2"),
    "n_4": ("h_1_0", "m_3"),
    "z": ("w_4",),
    "q_0": ("e",),
    "y_2": ("c_1",),
    "s_3": ("h_1_0",),
    "t_2": ("h_0_1",),
    "t_3": ("h_1_1",),
}
GRADS = (((0, 1), True), ((2,), True), ((3,), True), ((4,), False))
COST = 1
SHARDS = (
    (0, 0, 0), (0, 1, 0), (0, 0, 1), (0, 1, 1),
    (-1, 0, 0), (-1, 1, 0), (-1, 0, 1), (-1, 1, 1),
    (2, 0, 0), (2, 1, 0),
    (1, 0, 1), (1, 1, 1), (1, 0, 0), (1, 1, 0),
    (2, 0, 1), (2, 1, 1),
)
N_PIECES = 8
PIECE = 256
UNIT = 512
ROWS = N_PIECES * PIECE


def pairs(move):
    sizes = (2, 4, 4, 2, 2)

    def index(at):
        n = 0
        for i, size in zip(at, sizes):
            n = n * size + i % size
        return n

    out = []
    for n in range(128):
        rest, at = n, []
        for size in reversed(sizes):
            at.append(rest % size)
            rest //= size
        at = tuple(reversed(at))
        out.append((index(at), index(move(*at))))
    return out


def move(v, to, name):
    with jax.named_scope(name):
        return lax.ppermute(v, ("dp", "tensor"), pairs(to))


def along_x(v, name):
    return move(v, lambda yh, z, x, yl, c: (yh, z, x + 1 - 2 * c, yl, c), name)


def along_y(v, name):
    return move(v, lambda yh, z, x, yl, c: (yh, z, x, yl + 1, c), name)


def across_cores(v, name):
    return move(v, lambda yh, z, x, yl, c: (yh, z, x, yl, c + 1), name)


def along_z(v, step, name):
    return move(v, lambda yh, z, x, yl, c: (yh, z + step * (1 - 2 * c), x, yl, c), name)


def across_y(v, name):
    return move(v, lambda yh, z, x, yl, c: (yh + 1, z, x, yl, c), name)


def after(v, *others):
    return lax.optimization_barrier((v, *others))[0]


def after_all(values, *others):
    return lax.optimization_barrier((*values, *others))[: len(values)]


def cost(flops, bytes_accessed, transcendentals):
    return pl.CostEstimate(
        flops=int(COST * flops),
        bytes_accessed=int(COST * bytes_accessed),
        transcendentals=int(COST * transcendentals),
    )


def params():
    return pltpu.CompilerParams(vmem_limit_bytes=VMEM_LIMIT)


def hbm(values):
    return [pltpu.with_memory_space_constraint(v, pltpu.HBM) for v in values]


def vmem(values):
    return [pltpu.with_memory_space_constraint(v, pltpu.VMEM) for v in values]


IN_HBM = pl.BlockSpec(memory_space=pltpu.HBM)
IN_VMEM = pl.BlockSpec(memory_space=pltpu.VMEM)


def width(units):
    return sum(unit[3] for unit in units)


def columns(dests, first, units):
    at = 0
    for u, (_, _, start, size) in enumerate(units):
        yield slice(at, at + size), pl.ds(pl.multiple_of(dests[first + u] * UNIT + start, size), size)
        at += size


def first_unit(k):
    return sum(len(units) for units in CHUNKS[:k])


def slices_kernel(dests, cotangent, *refs):
    outs, sems = refs[:-1], refs[-1]
    copies = []
    for out, group in zip(outs, GROUPS):
        at = 0
        for k in group:
            for here, there in columns(dests, first_unit(k), CHUNKS[k]):
                copies.append(
                    pltpu.make_async_copy(
                        cotangent.at[:, there],
                        out.at[:, at + here.start : at + here.stop],
                        sems.at[len(copies)],
                    )
                )
            at += width(CHUNKS[k])
    for copy in copies:
        copy.start()
    for copy in copies:
        copy.wait()


def slices(dests, cotangent):
    rows = cotangent.shape[0]
    return pl.pallas_call(
        slices_kernel,
        grid_spec=pltpu.PrefetchScalarGridSpec(
            num_scalar_prefetch=1,
            grid=(),
            in_specs=[IN_HBM],
            out_specs=[IN_VMEM] * len(GROUPS),
            scratch_shapes=[pltpu.SemaphoreType.DMA((first_unit(len(CHUNKS)),))],
        ),
        out_shape=[
            pltpu.VMEM((rows, sum(width(CHUNKS[k]) for k in group)), BF16) for group in GROUPS
        ],
        compiler_params=params(),
        cost_estimate=cost(
            flops=0, bytes_accessed=2 * cotangent.size, transcendentals=0
        ),
        name="slices",
    )(dests, *hbm([cotangent]))


def pair_kernel(widths, mine, partner, *outs):
    rows = mine.shape[0]
    at = 0
    for out, n in zip(outs, widths):
        out[:rows] = mine[:, at : at + n]
        out[rows:] = partner[:, at : at + n]
        at += n


def pair_up(group, mine, partner):
    rows = mine.shape[0]
    widths = [width(CHUNKS[k]) for k in group]
    return pl.pallas_call(
        lambda *refs: pair_kernel(widths, *refs),
        in_specs=[IN_VMEM] * 2,
        out_specs=[IN_VMEM] * len(widths),
        out_shape=[pltpu.VMEM((2 * rows, n), BF16) for n in widths],
        compiler_params=params(),
        cost_estimate=cost(flops=0, bytes_accessed=4 * mine.size, transcendentals=0),
        name="pair_up",
    )(*vmem([mine, partner]))


GROUP = 4


def factors_kernel(order, lengths, remasked, *refs):
    gates, uppers = refs[:GROUP], refs[GROUP : 2 * GROUP]
    hidden_t, up_factor, gate_factor = refs[2 * GROUP :]
    rows = gates[0].shape[0]
    marks = remasked[...]
    for k in range(GROUP):
        shard = pl.program_id(0) * GROUP + k
        start = order[shard] * rows
        at = start + lax.broadcasted_iota(jnp.int32, (rows, marks.shape[1]), 0)
        marked = jnp.max(jnp.where(at == marks, 1.0, 0.0), axis=1, keepdims=True)
        position = start + lax.broadcasted_iota(jnp.int32, (rows, 1), 0)
        weight = jnp.where(position < lengths[0], 1.0 + marked, 0.0)
        gate_f = gates[k][...].astype(F32)
        upper_f = uppers[k][...].astype(F32)
        sigma = 0.5 + 0.5 * jnp.tanh(0.5 * gate_f)
        weighted = gate_f * sigma * weight
        at = pl.ds(pl.multiple_of(shard * rows, rows), rows)
        hidden_t[:, at] = (weighted * upper_f).astype(BF16).T
        up_factor[at] = weighted.astype(BF16)
        slope = (sigma * weight) * (1.0 + gate_f * (1.0 - sigma))
        gate_factor[at] = (upper_f * slope).astype(BF16)


def factors(order, lengths, remasked, gate, upper):
    rows, width = gate.shape
    block = rows // 16
    blocks = [
        pl.BlockSpec((block, width), lambda i, order, lengths, k=k: (order[i * GROUP + k], 0))
        for k in range(GROUP)
    ]
    return pl.pallas_call(
        factors_kernel,
        grid_spec=pltpu.PrefetchScalarGridSpec(
            num_scalar_prefetch=2,
            grid=(16 // GROUP,),
            in_specs=[pl.BlockSpec(remasked.shape, lambda i, order, lengths: (0, 0))] + blocks * 2,
            out_specs=[IN_VMEM] * 3,
        ),
        out_shape=[
            pltpu.VMEM((width, rows), BF16),
            pltpu.VMEM((rows, width), BF16),
            pltpu.VMEM((rows, width), BF16),
        ],
        compiler_params=params(),
        cost_estimate=cost(
            flops=30 * rows * width, bytes_accessed=4 * rows * width, transcendentals=rows * width
        ),
        name="factors",
    )(order, lengths, remasked, *hbm([gate] * GROUP), *hbm([upper] * GROUP))


def weight_kernel(n, flip, hidden_t, *refs):
    pieces, outs, chunk = refs[:N_PIECES], refs[N_PIECES : N_PIECES + n], refs[-1]
    size = chunk.shape[2]
    for u, out in enumerate(outs):
        at = pl.ds(pl.multiple_of(jnp.bitwise_xor(u, flip[0]) * size, size), size)
        for i, piece in enumerate(pieces):
            chunk[u, i * PIECE : (i + 1) * PIECE] = piece[:, at]
        out[...] = jnp.dot(hidden_t[...], chunk[u], preferred_element_type=F32).astype(BF16)


def weight_terms(flip, hidden_t, pieces, units):
    ff, rows = hidden_t.shape
    n = len(units)
    size = units[0][3]
    return pl.pallas_call(
        lambda *refs: weight_kernel(n, *refs),
        grid_spec=pltpu.PrefetchScalarGridSpec(
            num_scalar_prefetch=1,
            grid=(),
            in_specs=[IN_VMEM] * (1 + N_PIECES),
            out_specs=[IN_VMEM] * n,
            scratch_shapes=[pltpu.VMEM((n, rows, size), BF16)],
        ),
        out_shape=[pltpu.VMEM((ff, size), BF16)] * n,
        compiler_params=params(),
        cost_estimate=cost(
            flops=2 * ff * rows * n * size, bytes_accessed=2 * ff * n * size, transcendentals=0
        ),
        name="weight_terms",
    )(flip, *vmem([hidden_t, *pieces]))


BLOCK = 1024


def grad_kernel(ks, count, given, last, order, dests, *refs):
    refs = list(refs)
    chunks = [[refs.pop(0) for _ in range(count)] for _ in ks]
    weight = refs.pop(0)
    before = [refs.pop(0) for _ in range(given)]
    if last:
        up_factor, gate_factor, gate_out, up_out, *refs = refs
        gate_buf, up_buf, out_sems = refs[-3:]
    else:
        out = refs.pop(0)
    chunk, weights, sems = refs[:3]

    loads = []
    at = 0
    for k in ks:
        for here, there in columns(dests, first_unit(k), CHUNKS[k]):
            loads.append(
                pltpu.make_async_copy(
                    weight.at[:, there],
                    weights.at[:, at + here.start : at + here.stop],
                    sems.at[len(loads)],
                )
            )
            loads[-1].start()
        at += width(CHUNKS[k])

    shard = ROWS // 16
    stores = []
    for start in range(0, count * PIECE, BLOCK):
        for piece in range(start // PIECE, (start + BLOCK) // PIECE):
            at = 0
            for pieces in chunks:
                n = pieces[piece].shape[1]
                chunk[piece * PIECE : (piece + 1) * PIECE, at : at + n] = pieces[piece][...]
                at += n
        if start == 0:
            for load in loads:
                load.wait()
        rows = slice(start, start + BLOCK)
        total = lax.dot_general(
            chunk[rows], weights[...], (((1,), (1,)), ((), ())), preferred_element_type=F32
        )
        if given:
            per = before[0].shape[0]
            total += before[start // per][start % per : start % per + BLOCK]
        if not last:
            out[rows] = total
            continue
        gate_buf[rows] = (total * gate_factor[rows].astype(F32)).astype(BF16)
        up_buf[rows] = (total * up_factor[rows].astype(F32)).astype(BF16)
        for index in range(start // shard, (start + BLOCK) // shard):
            for which, (buf, result) in enumerate(((gate_buf, gate_out), (up_buf, up_out))):
                stores.append(
                    pltpu.make_async_copy(
                        buf.at[index * shard : (index + 1) * shard],
                        result.at[pl.ds(pl.multiple_of(order[index] * shard, shard), shard)],
                        out_sems.at[which, index],
                    )
                )
                stores[-1].start()
    for store in stores:
        store.wait()


def grad(order, dests, ks, chunks, weight, before=(), rest=()):
    ff = weight.shape[0]
    size = sum(width(CHUNKS[k]) for k in ks)
    count = len(chunks[0])
    rows = count * PIECE
    given, last = len(before), len(rest) > 0
    scratch = [
        pltpu.VMEM((rows, size), BF16),
        pltpu.VMEM((ff, size), BF16),
        pltpu.SemaphoreType.DMA((sum(len(CHUNKS[k]) for k in ks),)),
    ]
    if last:
        scratch += [pltpu.VMEM((rows, ff), BF16)] * 2
        scratch += [pltpu.SemaphoreType.DMA((2, 16))]
        out_specs = [IN_HBM] * 2
        out_shape = [jax.ShapeDtypeStruct((rows, ff), BF16)] * 2
    else:
        out_specs = IN_VMEM
        out_shape = pltpu.VMEM((rows, ff), F32)
    pieces = [p for chunk in chunks for p in chunk]
    rest = [*before, *rest]
    return pl.pallas_call(
        lambda *refs: grad_kernel(ks, count, given, last, *refs),
        grid_spec=pltpu.PrefetchScalarGridSpec(
            num_scalar_prefetch=2,
            grid=(),
            in_specs=[IN_VMEM] * len(pieces) + [IN_HBM] + [IN_VMEM] * len(rest),
            out_specs=out_specs,
            scratch_shapes=scratch,
        ),
        out_shape=out_shape,
        input_output_aliases={2 + len(pieces) + 1: 0} if given and not last else {},
        compiler_params=params(),
        cost_estimate=cost(
            flops=2 * rows * ff * size, bytes_accessed=2 * ff * size, transcendentals=0
        ),
        name="grad",
    )(order, dests, *vmem(pieces), *hbm([weight]), *vmem(rest))


def local(cotangent, gate_in, up_in, down_weight, lengths, remasked):
    t = lax.axis_index("tensor")
    d = lax.axis_index("dp")
    x, yl, c = t // 4, (t // 2) % 2, t % 2
    yh, z = d // 4, d % 4
    way = 1 - 2 * c
    order = jnp.stack(
        [
            (((x + way * dx + 4) % 4) * 2 + (yl + dy) % 2) * 2 + (c + dc) % 2
            for dx, dy, dc in SHARDS
        ]
    ).astype(jnp.int32)
    dests = jnp.stack(
        [((yh + dy) % 2) * 4 + (z + dz) % 4 for units in CHUNKS for dz, dy, _, _ in units]
    ).astype(jnp.int32)
    flip = c.astype(jnp.int32).reshape(1)
    straight = jnp.zeros((1,), jnp.int32)

    steps = Steps()

    def add(*terms):
        return sum(term.astype(F32) for term in terms)

    steps["i"] = lambda wait: slices(dests, wait(cotangent))
    steps["e"] = lambda wait: factors(wait(order), lengths, remasked, gate_in, up_in)
    for i, group in enumerate(GROUPS):
        steps[f"y_{i}"] = lambda wait, i=i: along_y(
            wait(steps["i"][i], *([steps[f"y_{i - 1}"]] if i else [])), f"y_{i}"
        )
        steps[f"q_{i}"] = lambda wait, i=i, group=group: pair_up(
            group, steps["i"][i], wait(steps[f"y_{i}"])
        )
        for j, k in enumerate(group):
            steps[f"p_{k}"] = lambda wait, i=i, j=j: steps[f"q_{i}"][j]
    for k in range(len(CHUNKS)):
        for name, source, call in (
            ("c", "p", across_cores),
            ("n", "p", along_x),
            ("m", "c", along_x),
            ("f", "n", along_x),
            ("s", "n", across_cores),
            ("t", "m", across_cores),
            ("u", "f", across_cores),
        ):
            steps[f"{name}_{k}"] = lambda wait, source=f"{source}_{k}", call=call, name=f"{name}_{k}": (
                call(wait(steps[source]), name)
            )
        steps[f"k_{k}"] = lambda wait, k=k: [
            steps[f"{name}_{k}"]
            for name in ("p", "c", "n", "m", "f", "s", "t", "u")
        ]
        steps[f"w_{k}"] = lambda wait, k=k: weight_terms(
            wait(flip if k in (1, 3) else straight),
            steps["e"][0],
            steps[f"k_{k}"],
            CHUNKS[k],
        )
    for i, (opposite, both) in enumerate(((0, 1), (2, 3))):
        steps[f"r_{i}"] = lambda wait, i=i, k=opposite: along_z(
            wait(steps[f"w_{k}"][0]), 1, f"r_{i}"
        )
        steps[f"b_{i}"] = lambda wait, i=i, k=both: along_z(
            wait(steps[f"w_{k}"][1]), -1, f"b_{i}"
        )
        steps[f"g_{i}"] = lambda wait, i=i, k=both: along_z(
            wait(add(steps[f"w_{k}"][0], steps[f"r_{i}"]).astype(BF16)), 1, f"g_{i}"
        )
    steps["o"] = lambda wait: across_y(
        wait(add(steps["w_2"][1], steps["b_0"], steps["g_0"]).astype(BF16)), "o"
    )
    for i, (ks, halves) in enumerate(GRADS[:-1]):
        for h in range(2 if halves else 1):

            def part(wait, i=i, ks=ks, halves=halves, h=h):
                chunks = [steps[f"k_{k}"] for k in ks]
                if halves:
                    chunks = [chunk[4 * h : 4 * h + 4] for chunk in chunks]
                before = grads_made(i - 1)
                before = before[h : h + 1] if halves else before
                return grad(order, wait(dests), ks, chunks, down_weight, before)

            steps[f"h_{i}_{h}"] = part

    def grads_made(i):
        return [steps[f"h_{i}_{h}"] for h in range(2 if GRADS[i][1] else 1)] if i >= 0 else []

    steps["z"] = lambda wait: grad(
        order, wait(dests), GRADS[-1][0], [steps[f"k_{k}"] for k in GRADS[-1][0]], down_weight,
        grads_made(len(GRADS) - 2), steps["e"][1:],
    )
    gate_grad, up_grad = steps["z"]
    terms = (steps["w_4"][0], steps["o"], steps["b_1"], steps["g_1"])
    return (gate_grad, up_grad, add(*terms))


class Steps:
    def __init__(self):
        self.rules, self.made, self.open = {}, {}, set()

    def __setitem__(self, name, rule):
        self.rules[name] = rule

    def __getitem__(self, name):
        if name not in self.made:
            if name in self.open:
                raise ValueError("circular wait")
            self.open.add(name)
            others = [self[other] for other in WAITS.get(name, ())]
            others = [v[0] if isinstance(v, (list, tuple)) else v for v in others]

            def wait(v, *more):
                return after(v, *others, *more) if others or more else v

            self.made[name] = self.rules[name](wait)
        return self.made[name]


def solution(mesh):
    return jax.shard_map(
        local,
        mesh=mesh,
        in_specs=(
            P(("dp", "tensor"), None),
            P("dp", "tensor"),
            P("dp", "tensor"),
            P("tensor", None),
            P("dp"),
            P("dp", None),
        ),
        out_specs=(P("dp", "tensor"), P("dp", "tensor"), P("tensor", "dp")),
        check_vma=False,
    )
```
